32 devices in a mesh: groups: 2 (over y), replica: 4 (over x, core), trow: 4 (over z).
Axes of the slice: x: 2, y: 2, z: 4, core: 2. Of those that a mesh axis runs over, the one named last changes fastest.
Arguments:
- hidden: bfloat16 [5120, 8192], P(('groups', 'replica'), 'trow'), parts along dimension 0, may hold values from -36 to 36, as said below
- w_query: bfloat16 [8192, 4096], P('replica', 'trow'), as said below
- w_keyval: bfloat16 [8192, 8, 256], P('replica', 'trow'), as said below
- seg_lengths: int32 [8, 2], P(('groups', 'replica')), parts along dimension 0, may hold values from 128 to 512, as said below
- home_pos: int32 [5120], P('groups'), parts along dimension 0, may hold values from 0 to 2559, as said below
Outputs:
- attended: bfloat16 [5120, 4096], P(('groups', 'replica'), 'trow'), parts along dimension 0
The draws below stay inside these ranges and needn't reach their ends.
There are 2 independent parts, one for each index of `groups`. The reference program is written for one: setup_inputs(seed, part) draws one part's arguments, and reference() takes and returns one part's arrays. A program takes and returns all parts, laid end to end along the dimension named above; an argument that names none is the same for every part. Nothing has to cross between parts.
Inputs may be any that keep to these rules, and one draw needn't show every extreme that they name: `hidden`: Floats. `w_query`: floats scaled by the inverse square root of 8192. `w_keyval`: floats scaled by the inverse square root of 8192. `seg_lengths`: each replica's 2 lengths sum to exactly 640; some replica has a segment of 512 tokens. `home_pos`: A permutation of the 2560 rows; the rows of each replica go in equal numbers to the home rows of every replica.
All inputs are finite; a program needn't handle non-finite values.
Results may differ from the reference program's by a relative error of at most 0.0068.
Values may be sent and summed in bfloat16 or wider, within the bound.
No kernel may reach another device: no remote copies, remote signals or barrier semaphores. Data moves between devices by JAX's collectives and lax.ppermute only.
A program may use at most 128 MiB of HBM per device.

```python
import math
import jax
import jax.numpy as jnp
from jax import lax

D = 8192
KVH = 8
HEAD = 128
QH = 32
SEGS = 2
AVG = 320
LONGEST = 512
TOK_HOME = 640
TOKENS = 2560
N_REPLICA = 4


def permute_rows(subkey):
    return jax.random.permutation(subkey, TOK_HOME).astype(jnp.int32)


def permute_segments(subkey):
    return jax.random.permutation(subkey, SEGS).astype(jnp.int32)


def draw_hidden(key, part):
    key = jax.random.fold_in(key, 3)
    first_key = jax.random.fold_in(key, 0)
    samples = jnp.clip(jax.random.normal(first_key, (TOKENS, D), jnp.float32), -6.0, 6.0)
    return samples.astype(jnp.bfloat16)


def draw_w_query(key, part):
    key = jax.random.fold_in(key, 11)
    noise = jax.random.normal(key, (D, KVH, QH // KVH, HEAD), jnp.float32)
    return (noise * D ** (-0.5)).reshape(D, QH * HEAD).astype(jnp.bfloat16)


def draw_w_keyval(key, part):
    key = jax.random.fold_in(key, 13)
    noise = jax.random.normal(key, (D, KVH, 2 * HEAD), jnp.float32)
    return (noise * D ** (-0.5)).astype(jnp.bfloat16)


def draw_seg_lengths(key, part):
    key = jax.random.fold_in(key, 7)
    offset_key, order_key = jax.random.split(key)
    spread = LONGEST - AVG
    offsets = jax.random.randint(offset_key, (N_REPLICA, SEGS // 2), -spread, spread + 1, dtype=jnp.int32)
    offsets = offsets.at[0, 0].set(spread)
    lengths = jnp.concatenate([AVG + offsets, AVG - offsets], axis=1)
    shuffles = jax.vmap(permute_segments)(jax.random.split(order_key, N_REPLICA))
    return jnp.take_along_axis(lengths, shuffles, axis=1).astype(jnp.int32)


def draw_home_pos(key, part):
    key = jax.random.fold_in(key, 9)
    rank_key, slot_key = jax.random.split(key)
    per_pair = TOK_HOME // N_REPLICA
    rank_table = jax.vmap(permute_rows)(jax.random.split(rank_key, N_REPLICA))
    owner_rep = rank_table // per_pair
    slot_index = jnp.arange(N_REPLICA, dtype=jnp.int32)[:, None] * per_pair + rank_table % per_pair
    slot_table = jax.vmap(permute_rows)(jax.random.split(slot_key, N_REPLICA))
    local_row = slot_table[owner_rep, slot_index]
    return (owner_rep * TOK_HOME + local_row).reshape(-1).astype(jnp.int32)


def setup_inputs(seed: int = 0, part: int = 0) -> dict:
    key_of = jax.random.split(jax.random.key(seed), 6)
    part_keys = jax.random.split(jax.random.fold_in(key_of[5], part), 6)
    return {
        "hidden": draw_hidden(jax.random.fold_in(jax.random.fold_in(key_of[5], part), 71), part),
        "w_query": draw_w_query(jax.random.fold_in(key_of[5], 71), part),
        "w_keyval": draw_w_keyval(jax.random.fold_in(key_of[5], 71), part),
        "seg_lengths": draw_seg_lengths(jax.random.fold_in(jax.random.fold_in(key_of[5], part), 71), part),
        "home_pos": draw_home_pos(jax.random.fold_in(jax.random.fold_in(key_of[5], part), 71), part),
    }


rope_base = 500000.0

def segment_layout(lengths_row, count):
    seg_ends = jnp.cumsum(lengths_row).astype(jnp.int32)
    seg_starts = seg_ends - lengths_row
    row_index = jnp.arange(count, dtype=jnp.int32)
    segment = lax.optimization_barrier(jnp.sum((row_index[:, None] >= seg_ends[None, :]).astype(jnp.int32), axis=1))
    picked = segment[:, None] == jnp.arange(lengths_row.shape[0], dtype=jnp.int32)[None, :]
    seg_first = lax.optimization_barrier(jnp.sum(jnp.where(picked, seg_starts[None, :], 0), axis=1)).astype(jnp.int32)
    return (segment, row_index - seg_first)

def rotate(vectors, position):
    half_dim = vectors.shape[-1] // 2
    exponent = jnp.arange(half_dim, dtype=jnp.float32) * (2.0 / vectors.shape[-1])
    frequency = jnp.power(jnp.float32(rope_base), -exponent)
    angle = position.astype(jnp.float32)[:, None] * frequency[None, :]
    cosine = jnp.cos(angle)[:, None, :]
    sine = jnp.sin(angle)[:, None, :]
    first_half = vectors[..., :half_dim]
    second_half = vectors[..., half_dim:]
    return jnp.concatenate([first_half * cosine - second_half * sine, second_half * cosine + first_half * sine], axis=-1)

def attend(query, keys, values, segment, count):
    head_dim = keys.shape[2]
    grouped = query.reshape(count, keys.shape[1], -1, head_dim)
    scores = jnp.einsum('qkgd,skd->kgqs', grouped.astype(jnp.float32), keys.astype(jnp.float32)) / math.sqrt(head_dim)
    row_index = jnp.arange(count, dtype=jnp.int32)
    allowed = (segment[:, None] == segment[None, :]) & (row_index[None, :] <= row_index[:, None])
    scores = jnp.where(allowed[None, None], scores, -jnp.inf)
    peak = lax.optimization_barrier(jnp.max(scores, axis=-1, keepdims=True))
    weights = jnp.exp(scores - peak)
    probs = (weights / lax.optimization_barrier(jnp.sum(weights, axis=-1, keepdims=True))).astype(jnp.bfloat16)
    mixed = jnp.einsum('kgqs,skd->qkgd', probs.astype(jnp.float32), values.astype(jnp.float32))
    return mixed.reshape(count, -1).astype(jnp.bfloat16)

def reference(hidden, w_query, w_keyval, seg_lengths, home_pos):
    flat_keyval = w_keyval.reshape(D, KVH * 2 * HEAD)

    def one_replica(replica_index):
        block = lax.dynamic_slice_in_dim(hidden, replica_index * TOK_HOME, TOK_HOME, 0)
        lengths_row = lax.dynamic_index_in_dim(seg_lengths, replica_index, 0, keepdims=False)
        segment, position = segment_layout(lengths_row, TOK_HOME)
        query_raw = jnp.dot(block, w_query, preferred_element_type=jnp.float32).reshape(TOK_HOME, QH, HEAD)
        keyval_raw = jnp.dot(block, flat_keyval, preferred_element_type=jnp.float32).reshape(TOK_HOME, KVH, 2 * HEAD)
        query = rotate(query_raw, position).astype(jnp.bfloat16)
        keys = rotate(keyval_raw[..., :HEAD], position).astype(jnp.bfloat16)
        values = keyval_raw[..., HEAD:].astype(jnp.bfloat16)
        return attend(query, keys, values, segment, TOK_HOME)
    packed = lax.map(one_replica, jnp.arange(N_REPLICA, dtype=jnp.int32))
    packed = packed.reshape(TOKENS, QH * HEAD)
    return jnp.zeros((TOKENS, QH * HEAD), jnp.bfloat16).at[home_pos].set(packed)
```

```python
import functools
import math

import jax
import jax.numpy as jnp
from jax import lax
from jax.experimental import pallas as pl
from jax.experimental.pallas import tpu as pltpu
from jax.sharding import PartitionSpec as P

rope_base = 500000.0
BF16 = jnp.bfloat16
F32 = jnp.float32
VMEM_BYTES = 56 * 1024 * 1024


def row_tables(lengths_row, count, head_dim):
    seg_ends = jnp.cumsum(lengths_row)
    seg_starts = seg_ends - lengths_row
    row_index = jnp.arange(count, dtype=jnp.int32)
    segment = jnp.sum((row_index[:, None] >= seg_ends[None, :]).astype(jnp.int32), axis=1)
    picked = segment[:, None] == jnp.arange(lengths_row.shape[0], dtype=jnp.int32)[None, :]
    seg_first = jnp.sum(jnp.where(picked, seg_starts[None, :], 0), axis=1)
    position = row_index - seg_first
    half_dim = head_dim // 2
    exponent = jnp.arange(half_dim, dtype=F32) * (2.0 / head_dim)
    frequency = jnp.power(F32(rope_base), -exponent)
    angle = position.astype(F32)[:, None] * frequency[None, :]
    cosine, sine = jnp.cos(angle), jnp.sin(angle)
    return (
        seg_first.astype(jnp.int32)[:, None],
        jnp.concatenate([cosine, cosine], axis=1),
        jnp.concatenate([-sine, sine], axis=1),
    )


def route_tables(home_pos, replicas, tok_rows, me):
    per_pair = tok_rows // replicas
    table = home_pos.reshape(replicas, tok_rows)
    owner = table // tok_rows
    kinds = jnp.arange(replicas, dtype=jnp.int32)
    onehot = owner[:, :, None] == kinds[None, None, :]
    row = jnp.arange(tok_rows, dtype=jnp.int32)
    earlier = (row[None, :] < row[:, None]).astype(BF16)
    counts = jnp.einsum("ij,sjo->sio", earlier, onehot.astype(BF16), preferred_element_type=F32)
    rank = jnp.sum(jnp.where(onehot, counts, 0.0), axis=2).astype(jnp.int32)
    my_owner = lax.dynamic_index_in_dim(owner, me, 0, keepdims=False)
    my_rank = lax.dynamic_index_in_dim(rank, me, 0, keepdims=False)
    slot = (my_owner ^ me) * per_pair + my_rank
    place = (kinds[:, None] ^ me) * per_pair + rank
    target = (table - me * tok_rows).reshape(-1)
    hit = target[None, :] == row[:, None]
    source = jnp.sum(jnp.where(hit, place.reshape(-1)[None, :], 0), axis=1)
    return slot.astype(jnp.int32)[None, :], source.astype(jnp.int32)[:, None]


def block_cols(q_cols, kv_cols):
    return math.gcd(512, q_cols, kv_cols)


def fetch(picks, step, wq, wkv, buf, sem, q_cols, block, slot):
    width = buf.shape[2]
    q_blocks = q_cols // width
    refs, first = (wq, block * width) if block < q_blocks else (wkv, (block - q_blocks) * width)

    def start():
        for j, ref in enumerate(refs):
            @pl.when(picks[step] == j)
            def _():
                pltpu.make_async_copy(ref.at[:, pl.ds(first, width)], buf.at[slot], sem.at[slot]).start()

    def wait():
        pltpu.make_async_copy(refs[0].at[:, pl.ds(first, width)], buf.at[slot], sem.at[slot]).wait()

    return start, wait


def project_kernel(steps, shards, q_cols, all_cols, picks, *refs):
    hidden, refs = refs[:steps], refs[steps:]
    wq, refs = refs[:shards], refs[shards:]
    wkv, refs = refs[:shards], refs[shards:]
    out, buf, sem = refs
    width = buf.shape[2]
    blocks = all_cols // width
    todo = [(block, step) for block in range(blocks) for step in range(steps)]
    copies = [
        fetch(picks, step, wq, wkv, buf, sem, q_cols, block, i % 3) for i, (block, step) in enumerate(todo)
    ]
    copies[0][0]()
    if len(todo) > 1:
        copies[1][0]()
    for i, (block, step) in enumerate(todo):
        if i + 2 < len(todo):
            copies[i + 2][0]()
        copies[i][1]()
        part = jnp.dot(hidden[step][...], buf[i % 3], preferred_element_type=F32)
        span = slice(block * width, (block + 1) * width)
        if step == 0:
            out[:, span] = part
        else:
            out[:, span] += part


def project(picks, hidden, wq, wkv):
    rows, depth = hidden[0].shape
    q_cols, kv_cols = wq[0].shape[1], wkv[0].shape[1]
    steps, shards = len(hidden), len(wq)
    vmem = pl.BlockSpec(memory_space=pltpu.VMEM)
    hbm = pl.BlockSpec(memory_space=pl.ANY)
    return pl.pallas_call(
        functools.partial(project_kernel, steps, shards, q_cols, q_cols + kv_cols),
        out_shape=jax.ShapeDtypeStruct((rows, q_cols + kv_cols), F32),
        in_specs=[pl.BlockSpec(memory_space=pltpu.SMEM)] + [vmem] * steps + [hbm] * (2 * shards),
        out_specs=vmem,
        scratch_shapes=[pltpu.VMEM((3, depth, block_cols(q_cols, kv_cols)), BF16), pltpu.SemaphoreType.DMA((3,))],
        compiler_params=pltpu.CompilerParams(vmem_limit_bytes=VMEM_BYTES),
        cost_estimate=pl.CostEstimate(
            flops=2 * rows * depth * steps * (q_cols + kv_cols), bytes_accessed=30_000_000, transcendentals=0
        ),
        name="project",
    )(picks, *hidden, *wq, *wkv)


def attend_kernel(shards, earlier, last, heads, kv_heads, head_dim, picks, *refs):
    part, refs = refs[0], refs[1:]
    wq, refs = refs[:shards], refs[shards:]
    wkv, refs = refs[:shards], refs[shards:]
    raw_in, cos_ref, sin_ref, first_ref, refs = *refs[:4], refs[4:]
    if earlier:
        kv_before, refs = refs[0], refs[1:]
    if last:
        mixed_before, slot_ref, refs = *refs[:2], refs[2:]
        out_refs, refs = refs[:-4], refs[-4:]
    else:
        kv_out, mixed_ref, refs = *refs[:2], refs[2:]
    buf, sem, raw, kv_all = refs[:4]
    rows = part.shape[0]
    q_cols = heads * head_dim
    all_cols = q_cols + 2 * kv_heads * head_dim
    group = heads // kv_heads
    width = buf.shape[2]
    blocks = all_cols // width
    copies = [fetch(picks, 0, wq, wkv, buf, sem, q_cols, block, block) for block in range(blocks)]
    for start, _ in copies:
        start()
    if earlier:
        kv_all[0:earlier] = kv_before[...]
    cos, sin = cos_ref[...], sin_ref[...]

    def rotated(first):
        u = raw[:, first : first + head_dim]
        return u * cos + pltpu.roll(u, head_dim // 2, 1) * sin

    for block, (_, wait) in enumerate(copies):
        wait()
        span = slice(block * width, (block + 1) * width)
        raw[:, span] = raw_in[:, span] + jnp.dot(part[...], buf[block], preferred_element_type=F32)
    here = slice(earlier, earlier + rows)
    for g in range(kv_heads):
        first = q_cols + 2 * g * head_dim
        kv_all[here, 2 * g * head_dim : (2 * g + 1) * head_dim] = rotated(first).astype(BF16)
        kv_all[here, (2 * g + 1) * head_dim : (2 * g + 2) * head_dim] = raw[
            :, first + head_dim : first + 2 * head_dim
        ].astype(BF16)
    if not last:
        kv_out[...] = kv_all[here]
    step = 256 if rows % 256 == 0 else rows
    scale = math.log2(math.e) / math.sqrt(head_dim)
    pieces = []
    for top in range(0, rows, step):
        span = earlier + top + step
        row_index = earlier + top + lax.broadcasted_iota(jnp.int32, (step, span), 0)
        key_index = lax.broadcasted_iota(jnp.int32, (step, span), 1)
        allowed = (key_index <= row_index) & (key_index >= first_ref[top : top + step])
        for h in range(heads):
            g = h // group
            u = raw[top : top + step, h * head_dim : (h + 1) * head_dim]
            q = u * cos[top : top + step] + pltpu.roll(u, head_dim // 2, 1) * sin[top : top + step]
            keys = kv_all[0:span, 2 * g * head_dim : (2 * g + 1) * head_dim]
            values = kv_all[0:span, (2 * g + 1) * head_dim : (2 * g + 2) * head_dim]
            scores = lax.dot_general(
                q.astype(BF16), keys, (((1,), (1,)), ((), ())), preferred_element_type=F32
            )
            scores = jnp.where(allowed, scores * scale, -jnp.inf)
            weights = jnp.exp2(scores - jnp.max(scores, axis=1, keepdims=True))
            total = jnp.sum(weights, axis=1, keepdims=True)
            mixed = jnp.dot(weights.astype(BF16), values, preferred_element_type=F32) / total
            if last:
                pieces.append(mixed.astype(BF16))
            else:
                mixed_ref[top : top + step, h * head_dim : (h + 1) * head_dim] = mixed.astype(BF16)
    if last:
        count = earlier + rows
        per = count // len(out_refs)
        for j, out in enumerate(out_refs):
            slots = j * per + lax.broadcasted_iota(jnp.int32, (per, count), 0)
            onehot = (slots == slot_ref[...]).astype(BF16)
            old = jnp.dot(onehot[:, :earlier], mixed_before[...], preferred_element_type=F32)
            for h in range(heads):
                span = slice(h * head_dim, (h + 1) * head_dim)
                new = jnp.dot(onehot[:, earlier:], pieces[h], preferred_element_type=F32)
                out[:, span] = (old[:, span] + new).astype(BF16)


def attend(picks, part, wq, wkv, raw, tables, earlier, head_dim, kv_before=None, mixed_before=None, slot=None, replicas=0):
    rows, depth = part.shape
    shards = len(wq)
    q_cols, kv_cols = wq[0].shape[1], wkv[0].shape[1]
    heads, kv_heads = q_cols // head_dim, kv_cols // (2 * head_dim)
    last = slot is not None
    count = earlier + rows
    vmem = pl.BlockSpec(memory_space=pltpu.VMEM)
    hbm = pl.BlockSpec(memory_space=pl.ANY)
    args = [part, *wq, *wkv, raw, tables[1], tables[2], tables[0]]
    specs = [vmem] + [hbm] * (2 * shards) + [vmem] * 4
    if earlier:
        args.append(kv_before)
        specs.append(vmem)
    if last:
        args += [mixed_before, slot]
        specs += [vmem] * 2
        outs = [jax.ShapeDtypeStruct((count // replicas, q_cols), BF16)] * replicas
    else:
        outs = [
            jax.ShapeDtypeStruct((rows, kv_cols), BF16),
            jax.ShapeDtypeStruct((rows, q_cols), BF16),
        ]
    width = block_cols(q_cols, kv_cols)
    blocks = (q_cols + kv_cols) // width
    return pl.pallas_call(
        functools.partial(attend_kernel, shards, earlier, last, heads, kv_heads, head_dim),
        out_shape=outs,
        in_specs=[pl.BlockSpec(memory_space=pltpu.SMEM)] + specs,
        out_specs=[vmem] * len(outs),
        scratch_shapes=[
            pltpu.VMEM((blocks, depth, width), BF16),
            pltpu.SemaphoreType.DMA((blocks,)),
            pltpu.VMEM((rows, q_cols + kv_cols), F32),
            pltpu.VMEM((count, kv_cols), BF16),
        ],
        compiler_params=pltpu.CompilerParams(vmem_limit_bytes=VMEM_BYTES),
        cost_estimate=pl.CostEstimate(
            flops=2 * rows * depth * (q_cols + kv_cols) + 4 * rows * count * q_cols,
            bytes_accessed=15_000_000,
            transcendentals=heads * rows * count,
        ),
        name="attend_last" if last else "attend_first",
    )(picks, *args)


def place_kernel(source_ref, *refs):
    blocks, out = refs[:-1], refs[-1]
    per = blocks[0].shape[0]
    rows = out.shape[0]
    total = None
    for j, block in enumerate(blocks):
        slots = j * per + lax.broadcasted_iota(jnp.int32, (rows, per), 1)
        onehot = (slots == source_ref[...]).astype(BF16)
        part = jnp.dot(onehot, block[...], preferred_element_type=F32)
        total = part if total is None else total + part
    out[...] = total.astype(BF16)


def place(source, blocks):
    vmem = pl.BlockSpec(memory_space=pltpu.VMEM)
    rows, cols = source.shape[0], blocks[0].shape[1]
    return pl.pallas_call(
        place_kernel,
        out_shape=jax.ShapeDtypeStruct((rows, cols), BF16),
        in_specs=[vmem] * (1 + len(blocks)),
        out_specs=vmem,
        compiler_params=pltpu.CompilerParams(vmem_limit_bytes=VMEM_BYTES),
        cost_estimate=pl.CostEstimate(flops=2 * rows * rows * cols, bytes_accessed=4 * rows * cols, transcendentals=0),
        name="place",
    )(source, *blocks)


def local(hidden, w_query, w_keyval, seg_lengths, home_pos):
    tok_rows, depth = hidden.shape
    w_rows = w_query.shape[0]
    head_dim = w_keyval.shape[2] // 2
    replicas, columns = lax.axis_size("replica"), lax.axis_size("trow")
    me, my_col = lax.axis_index("replica"), lax.axis_index("trow")
    flat_keyval = w_keyval.reshape(w_rows, -1)

    def swap(block, j):
        return lax.ppermute(block, "replica", [(i, i ^ j) for i in range(replicas)])

    ring = [(i, (i + 1) % columns) for i in range(columns)]
    cut = tok_rows * 4 // 5
    hiddens = [hidden]
    for _ in range(columns - 2):
        hiddens.append(lax.ppermute(hiddens[-1], "trow", ring))
    first_part = lax.ppermute(hiddens[-1][:cut], "trow", ring)
    last_part = lax.ppermute(hiddens[-1][cut:], "trow", ring)
    shard_of = [lax.rem(my_col - k + columns, columns) for k in range(columns)]
    if replicas == columns and replicas == 4:
        wq = [w_query, swap(w_query, 1), swap(w_query, 2)]
        wkv = [flat_keyval, swap(flat_keyval, 1), swap(flat_keyval, 2)]
        wq.append(swap(wq[2], 1))
        wkv.append(swap(wkv[2], 1))
        picks = [s ^ me for s in shard_of]
    else:
        all_q = lax.all_gather(w_query, "replica", axis=0, tiled=True)
        all_kv = lax.all_gather(flat_keyval, "replica", axis=0, tiled=True)
        wq = [all_q[s * depth : (s + 1) * depth] for s in range(columns)]
        wkv = [all_kv[s * depth : (s + 1) * depth] for s in range(columns)]
        picks = shard_of
    picks = jnp.stack(picks).astype(jnp.int32)

    seg_first, cosine, sine = row_tables(seg_lengths[0], tok_rows, head_dim)
    slot, source = route_tables(home_pos, replicas, tok_rows, me)
    raw = project(picks[:-1], hiddens, wq, wkv)
    kv_first, mixed_first = attend(
        picks[-1:], first_part, wq, wkv, raw[:cut], (seg_first[:cut], cosine[:cut], sine[:cut]), 0, head_dim
    )
    outgoing = attend(
        picks[-1:], last_part, wq, wkv, raw[cut:], (seg_first[cut:], cosine[cut:], sine[cut:]), cut, head_dim,
        kv_before=kv_first, mixed_before=mixed_first, slot=slot, replicas=replicas,
    )
    incoming = [outgoing[0]] + [swap(outgoing[j], j) for j in range(1, replicas)]
    return place(source, incoming)


def solution(mesh):
    placed = (
        P(("groups", "replica"), "trow"),
        P("replica", "trow"),
        P("replica", "trow", None),
        P(("groups", "replica"), None),
        P("groups"),
    )
    return jax.shard_map(
        local,
        mesh=mesh,
        in_specs=placed,
        out_specs=P(("groups", "replica"), "trow"),
        check_vma=False,
    )
```

```python
import functools
import math

import jax
import jax.numpy as jnp
from jax import lax
from jax.experimental import pallas as pl
from jax.experimental.pallas import tpu as pltpu
from jax.sharding import PartitionSpec as P

rope_base = 500000.0
BF16 = jnp.bfloat16
F32 = jnp.float32
VMEM_BYTES = 56 * 1024 * 1024
ROW_CHUNKS = (320, 192, 128)
VMEM = pl.BlockSpec(memory_space=pltpu.VMEM)
SMEM = pl.BlockSpec(memory_space=pltpu.SMEM)
HBM = pl.BlockSpec(memory_space=pl.ANY)


def row_tables(lengths_row, count, head_dim):
    seg_ends = jnp.cumsum(lengths_row)
    seg_starts = seg_ends - lengths_row
    row_index = jnp.arange(count, dtype=jnp.int32)
    segment = jnp.sum((row_index[:, None] >= seg_ends[None, :]).astype(jnp.int32), axis=1)
    picked = segment[:, None] == jnp.arange(lengths_row.shape[0], dtype=jnp.int32)[None, :]
    seg_first = jnp.sum(jnp.where(picked, seg_starts[None, :], 0), axis=1)
    position = row_index - seg_first
    half_dim = head_dim // 2
    exponent = jnp.arange(half_dim, dtype=F32) * (2.0 / head_dim)
    frequency = jnp.power(F32(rope_base), -exponent)
    angle = position.astype(F32)[:, None] * frequency[None, :]
    cosine, sine = jnp.cos(angle), jnp.sin(angle)
    return (
        seg_first.astype(jnp.int32)[:, None],
        jnp.concatenate([cosine, cosine], axis=1),
        jnp.concatenate([-sine, sine], axis=1),
    )


def home_sources(home_pos, tok_rows, me):
    target = home_pos - me * tok_rows
    hit = target[None, :] == jnp.arange(tok_rows, dtype=jnp.int32)[:, None]
    packed = jnp.arange(home_pos.shape[0], dtype=jnp.int32)
    return jnp.sum(jnp.where(hit, packed[None, :], 0), axis=1).astype(jnp.int32)[:, None]


class Weights:
    def __init__(self, query, keyval):
        self.query, self.keyval = query, keyval
        self.depth = keyval[0].shape[0]
        self.q_cols, self.kv_cols = query[0][0].shape[1], keyval[0].shape[1]
        self.all_cols = self.q_cols + self.kv_cols
        self.width = math.gcd(512, self.q_cols, self.kv_cols)
        self.blocks = self.all_cols // self.width

    def arrays(self):
        return [piece for pieces in self.query for piece in pieces] + self.keyval

    def refs(self, flat):
        flat = list(flat)
        query = [[flat.pop(0) for _ in pieces] for pieces in self.query]
        return query, flat

    def fetch(self, refs, pick, which, block, buf, sem):
        query, keyval = refs
        q_blocks = self.q_cols // self.width
        is_query = block < q_blocks
        span = pl.ds((block if is_query else block - q_blocks) * self.width, self.width)

        def start():
            for j in range(len(keyval)):
                pieces = query[j] if is_query else [keyval[j]]

                @pl.when(pick == j)
                def _(pieces=pieces):
                    if len(pieces) == 1:
                        pltpu.make_async_copy(pieces[0].at[:, span], buf, sem).start()
                    else:
                        half = self.depth // 2
                        for order in range(2):
                            @pl.when(which == order)
                            def _(order=order):
                                for n, piece in enumerate(pieces):
                                    rows = pl.ds((n ^ order) * half, half)
                                    pltpu.make_async_copy(piece.at[:, span], buf.at[rows], sem).start()

        def wait():
            whole = query[0][0] if is_query else keyval[0]
            pltpu.make_async_copy(whole.at[:, span], buf, sem).wait()

        return start, wait


def project_kernel(w, steps, chunks, ctrl, *refs):
    hidden, refs = refs[:steps], refs[steps:]
    count = len(w.arrays())
    w_refs, refs = w.refs(refs[:count]), refs[count:]
    outs, (held, buf, sem, h_sem) = refs[: len(chunks)], refs[len(chunks) :]
    which = ctrl[steps + 1]
    loads = [pltpu.make_async_copy(hidden[s], held.at[s], h_sem.at[s]) for s in range(steps)]
    todo = [(block, step) for block in range(w.blocks) for step in range(steps)]
    slots = buf.shape[0]
    copies = [
        w.fetch(w_refs, ctrl[step], which, block, buf.at[i % slots], sem.at[i % slots])
        for i, (block, step) in enumerate(todo)
    ]
    loads[0].start()
    for i in range(min(slots - 1, len(todo))):
        copies[i][0]()
        if i + 1 < steps:
            loads[i + 1].start()
    for s in range(min(slots, len(todo) + 1), steps):
        loads[s].start()
    for i, (block, step) in enumerate(todo):
        if i + slots - 1 < len(todo):
            copies[i + slots - 1][0]()
        if block == 0:
            loads[step].wait()
        copies[i][1]()
        span = slice(block * w.width, (block + 1) * w.width)
        first = 0
        for out, rows in zip(outs, chunks):
            part = jnp.dot(held[step, first : first + rows], buf[i % slots], preferred_element_type=F32)
            if step == 0:
                out[:, span] = part
            else:
                out[:, span] += part
            first += rows


def project(ctrl, hidden, w, chunks):
    rows, depth = hidden[0].shape
    steps = len(hidden)
    return pl.pallas_call(
        functools.partial(project_kernel, w, steps, chunks),
        out_shape=[jax.ShapeDtypeStruct((r, w.all_cols), F32) for r in chunks],
        in_specs=[SMEM] + [HBM] * (steps + len(w.arrays())),
        out_specs=[VMEM] * len(chunks),
        scratch_shapes=[
            pltpu.VMEM((steps, rows, depth), BF16),
            pltpu.VMEM((4, depth, w.width), BF16),
            pltpu.SemaphoreType.DMA((4,)),
            pltpu.SemaphoreType.DMA((steps,)),
        ],
        compiler_params=pltpu.CompilerParams(vmem_limit_bytes=VMEM_BYTES),
        cost_estimate=pl.CostEstimate(
            flops=2 * rows * depth * steps * w.all_cols, bytes_accessed=30_000_000, transcendentals=0
        ),
        name="project",
    )(ctrl, *hidden, *w.arrays())


def attend_kernel(w, last_step, heads, head_dim, before, ctrl, part, *refs):
    count = len(w.arrays())
    w_refs, refs = w.refs(refs[:count]), refs[count:]
    raw_in, cos_ref, sin_ref, first_ref, refs = *refs[:4], refs[4:]
    kv_before, refs = refs[: len(before)], refs[len(before) :]
    kv_out, mixed_ref, buf, sem, raw, kv_all = refs
    rows, earlier = part.shape[0], sum(before)
    kv_heads = w.kv_cols // (2 * head_dim)
    group = heads // kv_heads
    copies = [
        w.fetch(w_refs, ctrl[last_step], ctrl[last_step + 1], block, buf.at[block], sem.at[block])
        for block in range(w.blocks)
    ]
    for start, _ in copies[::-1]:
        start()
    top = 0
    for ref, n in zip(kv_before, before):
        kv_all[top : top + n] = ref[...]
        top += n
    cos, sin = cos_ref[...], sin_ref[...]

    def rotated(first):
        u = raw[:, first : first + head_dim]
        return (u * cos + pltpu.roll(u, head_dim // 2, 1) * sin).astype(BF16)

    for block in range(w.blocks)[::-1]:
        copies[block][1]()
        span = slice(block * w.width, (block + 1) * w.width)
        raw[:, span] = raw_in[:, span] + jnp.dot(part[...], buf[block], preferred_element_type=F32)
    here = slice(earlier, earlier + rows)
    for g in range(kv_heads):
        first = w.q_cols + 2 * g * head_dim
        kv_all[here, 2 * g * head_dim : (2 * g + 1) * head_dim] = rotated(first)
        kv_all[here, (2 * g + 1) * head_dim : (2 * g + 2) * head_dim] = raw[
            :, first + head_dim : first + 2 * head_dim
        ].astype(BF16)
    kv_out[...] = kv_all[here]
    span = earlier + rows
    row_index = earlier + lax.broadcasted_iota(jnp.int32, (rows, span), 0)
    key_index = lax.broadcasted_iota(jnp.int32, (rows, span), 1)
    allowed = (key_index <= row_index) & (key_index >= first_ref[...])
    scale = math.log2(math.e) / math.sqrt(head_dim)
    for h in range(heads):
        g = h // group
        keys = kv_all[0:span, 2 * g * head_dim : (2 * g + 1) * head_dim]
        values = kv_all[0:span, (2 * g + 1) * head_dim : (2 * g + 2) * head_dim]
        scores = lax.dot_general(
            rotated(h * head_dim), keys, (((1,), (1,)), ((), ())), preferred_element_type=F32
        )
        scores = jnp.where(allowed, scores * scale, -jnp.inf)
        weights = jnp.exp2(scores - jnp.max(scores, axis=1, keepdims=True))
        total = jnp.sum(weights, axis=1, keepdims=True)
        mixed = jnp.dot(weights.astype(BF16), values, preferred_element_type=F32) / total
        mixed_ref[:, h * head_dim : (h + 1) * head_dim] = mixed.astype(BF16)


def attend(ctrl, last_step, part, w, raw, tables, kv_before, head_dim):
    rows, depth = part.shape
    heads = w.q_cols // head_dim
    before = [a.shape[0] for a in kv_before]
    count = sum(before) + rows
    return pl.pallas_call(
        functools.partial(attend_kernel, w, last_step, heads, head_dim, before),
        out_shape=[
            jax.ShapeDtypeStruct((rows, w.kv_cols), BF16),
            jax.ShapeDtypeStruct((rows, w.q_cols), BF16),
        ],
        in_specs=[SMEM, VMEM] + [HBM] * len(w.arrays()) + [VMEM] * (4 + len(before)),
        out_specs=[VMEM] * 2,
        scratch_shapes=[
            pltpu.VMEM((w.blocks, depth, w.width), BF16),
            pltpu.SemaphoreType.DMA((w.blocks,)),
            pltpu.VMEM((rows, w.all_cols), F32),
            pltpu.VMEM((count, w.kv_cols), BF16),
        ],
        compiler_params=pltpu.CompilerParams(vmem_limit_bytes=VMEM_BYTES),
        cost_estimate=pl.CostEstimate(
            flops=2 * rows * depth * w.all_cols + 4 * rows * count * w.q_cols,
            bytes_accessed=15_000_000,
            transcendentals=heads * rows * count,
        ),
        name="attend",
    )(ctrl, part, *w.arrays(), raw, tables[1], tables[2], tables[0], *kv_before)


def place_kernel(tops, tok_rows, more, me_ref, source_ref, *refs):
    blocks, out = refs[: len(refs) - 1 - more], refs[-1]
    rows = out.shape[0]
    peers = len(blocks) // len(tops)
    me = me_ref[0]
    total = None
    for n, block in enumerate(blocks):
        chunk, j = divmod(n, peers)
        base = (me ^ j) * tok_rows + tops[chunk]
        index = lax.broadcasted_iota(jnp.int32, (rows, block.shape[0]), 1)
        onehot = (index == source_ref[...] - base).astype(BF16)
        part = jnp.dot(onehot, block[...], preferred_element_type=F32)
        total = part if total is None else total + part
    if more:
        total = total + refs[len(blocks)][...].astype(F32)
    out[...] = total.astype(BF16)


def place(me, source, blocks, tops, tok_rows, before=None):
    rows, cols = source.shape[0], blocks[0].shape[1]
    more = [] if before is None else [before]
    return pl.pallas_call(
        functools.partial(place_kernel, tops, tok_rows, len(more)),
        out_shape=jax.ShapeDtypeStruct((rows, cols), BF16),
        in_specs=[SMEM] + [VMEM] * (1 + len(blocks) + len(more)),
        out_specs=VMEM,
        compiler_params=pltpu.CompilerParams(vmem_limit_bytes=VMEM_BYTES),
        cost_estimate=pl.CostEstimate(
            flops=2 * rows * cols * sum(b.shape[0] for b in blocks),
            bytes_accessed=8 * rows * cols,
            transcendentals=0,
        ),
        name="place",
    )(me, source, *blocks, *more)


def local(hidden, w_query, w_keyval, seg_lengths, home_pos):
    tok_rows = hidden.shape[0]
    w_rows = w_query.shape[0]
    head_dim = w_keyval.shape[2] // 2
    replicas, columns = lax.axis_size("replica"), lax.axis_size("trow")
    me, my_col, my_group = lax.axis_index("replica"), lax.axis_index("trow"), lax.axis_index("groups")
    flat_keyval = w_keyval.reshape(w_rows, -1)
    total = sum(ROW_CHUNKS)
    chunks = [tok_rows * c // total for c in ROW_CHUNKS]
    tops = [sum(chunks[:n]) for n in range(len(chunks))]

    def swap(block, j):
        return lax.ppermute(block, "replica", [(i, i ^ j) for i in range(replicas)])

    def on(block):
        return lax.ppermute(block, "trow", [(i, (i + 1) % columns) for i in range(columns)])

    small = replicas == 4 and columns == 4
    if small:
        half = w_rows // 2
        h1 = on(hidden)
        mine = swap(lax.dynamic_slice_in_dim(w_query, my_group * half, half, 0), 2)
        query_1, keyval_1 = swap(w_query, 1), swap(flat_keyval, 1)
        h1, mine, keyval_later = lax.optimization_barrier((h1, mine, flat_keyval))
        h2 = on(h1)
        other = lax.ppermute(mine, "groups", [(0, 1), (1, 0)])
        keyval_2 = swap(keyval_later, 2)
        mine_3 = swap(mine, 1)
        h2, other, keyval_2 = lax.optimization_barrier((h2, other, keyval_2))
        hiddens = [hidden, h1, h2]
        parts = [on(h2[top : top + rows]) for top, rows in zip(tops, chunks)]
        weights = Weights(
            [[w_query], [query_1], [mine, other], [mine_3, swap(other, 1)]],
            [flat_keyval, keyval_1, keyval_2, swap(keyval_2, 1)],
        )
    else:
        hiddens = [hidden]
        for _ in range(columns - 2):
            hiddens.append(on(hiddens[-1]))
        parts = [on(hiddens[-1][top : top + rows]) for top, rows in zip(tops, chunks)]
        depth = hidden.shape[1]
        all_q = lax.all_gather(w_query, "replica", axis=0, tiled=True)
        all_kv = lax.all_gather(flat_keyval, "replica", axis=0, tiled=True)
        spans = [slice(s * depth, (s + 1) * depth) for s in range(columns)]
        weights = Weights([[all_q[s]] for s in spans], [all_kv[s] for s in spans])
    shard_of = [lax.rem(my_col - k + columns, columns) for k in range(columns)]
    picks = [s ^ me for s in shard_of] if small else shard_of
    ctrl = jnp.stack(picks + [my_group]).astype(jnp.int32)

    seg_first, cosine, sine = row_tables(seg_lengths[0], tok_rows, head_dim)
    source = home_sources(home_pos, tok_rows, me)
    me_array = me.astype(jnp.int32)[None]
    raws = project(ctrl, hiddens, weights, chunks)
    kv, mixed = [], []
    for part, raw, top, rows in zip(parts, raws, tops, chunks):
        tables = [t[top : top + rows] for t in (seg_first, cosine, sine)]
        kv_new, mixed_new = attend(ctrl, columns - 1, part, weights, raw, tables, kv, head_dim)
        kv, mixed = kv + [kv_new], mixed + [mixed_new]
    blocks = []
    for n, block in enumerate(mixed):
        if small:
            across = swap(block, 2)
            there = across
            if n + 1 < len(mixed):
                there, _ = lax.optimization_barrier((across, mixed[n + 1]))
            blocks.append([block, swap(block, 1), there, swap(there, 1)])
        else:
            blocks.append([block] + [swap(block, j) for j in range(1, replicas)])
    source_late, _ = lax.optimization_barrier((source, mixed[-1]))
    placed = place(me_array, source_late, sum(blocks[:-1], []), tops[:-1], tok_rows)
    return place(me_array, source_late, blocks[-1], tops[-1:], tok_rows, placed)


def solution(mesh):
    placed = (
        P(("groups", "replica"), "trow"),
        P("replica", "trow"),
        P("replica", "trow", None),
        P(("groups", "replica"), None),
        P("groups"),
    )
    return jax.shard_map(
        local,
        mesh=mesh,
        in_specs=placed,
        out_specs=P(("groups", "replica"), "trow"),
        check_vma=False,
    )
```

```python
import functools
import math

import jax
import jax.numpy as jnp
from jax import lax
from jax.experimental import pallas as pl
from jax.experimental.pallas import tpu as pltpu
from jax.sharding import PartitionSpec as P

rope_base = 500000.0
BF16 = jnp.bfloat16
F32 = jnp.float32
MIB = 1024 * 1024
PLACE_STEPS = 2
LANES = 128
ROW_CHUNKS = (320, 192, 128)
VMEM = pl.BlockSpec(memory_space=pltpu.VMEM)
SMEM = pl.BlockSpec(memory_space=pltpu.SMEM)
HBM = pl.BlockSpec(memory_space=pl.ANY)


def row_tables(lengths_row, count, head_dim):
    seg_ends = jnp.cumsum(lengths_row)
    seg_starts = seg_ends - lengths_row
    row_index = jnp.arange(count, dtype=jnp.int32)
    segment = jnp.sum((row_index[:, None] >= seg_ends[None, :]).astype(jnp.int32), axis=1)
    picked = segment[:, None] == jnp.arange(lengths_row.shape[0], dtype=jnp.int32)[None, :]
    seg_first = jnp.sum(jnp.where(picked, seg_starts[None, :], 0), axis=1)
    position = row_index - seg_first
    half_dim = head_dim // 2
    exponent = jnp.arange(half_dim, dtype=F32) * (2.0 / head_dim)
    frequency = jnp.power(F32(rope_base), -exponent)
    angle = position.astype(F32)[:, None] * frequency[None, :]
    cosine, sine = jnp.cos(angle), jnp.sin(angle)
    return (
        jnp.broadcast_to(seg_first.astype(jnp.int32)[:, None], (count, LANES)),
        jnp.concatenate([cosine, cosine], axis=1),
        jnp.concatenate([-sine, sine], axis=1),
    )


def home_sources(home_pos, tok_rows, me):
    target = home_pos - me * tok_rows
    hit = target[None, :] == jnp.arange(tok_rows, dtype=jnp.int32)[:, None]
    packed = jnp.arange(home_pos.shape[0], dtype=jnp.int32)
    source = jnp.sum(jnp.where(hit, packed[None, :], 0), axis=1).astype(jnp.int32)
    return jnp.broadcast_to(source[:, None], (tok_rows, LANES))


class Weights:
    def __init__(self, query, keyval):
        self.query, self.keyval = query, keyval
        self.depth = keyval[0].shape[0]
        self.q_cols, self.kv_cols = query[0][0].shape[1], keyval[0].shape[1]
        self.all_cols = self.q_cols + self.kv_cols
        self.width = math.gcd(512, self.q_cols, self.kv_cols)
        self.blocks = self.all_cols // self.width

    def arrays(self):
        return [piece for pieces in self.query for piece in pieces] + self.keyval

    def refs(self, flat):
        flat = list(flat)
        query = [[flat.pop(0) for _ in pieces] for pieces in self.query]
        return query, flat

    def fetch(self, refs, pick, which, block, buf, sem):
        query, keyval = refs
        q_blocks = self.q_cols // self.width
        is_query = block < q_blocks
        span = pl.ds((block if is_query else block - q_blocks) * self.width, self.width)

        def start():
            for j in range(len(keyval)):
                pieces = query[j] if is_query else [keyval[j]]

                @pl.when(pick == j)
                def _(pieces=pieces):
                    if len(pieces) == 1:
                        pltpu.make_async_copy(pieces[0].at[:, span], buf, sem).start()
                    else:
                        half = self.depth // 2
                        for order in range(2):
                            @pl.when(which == order)
                            def _(order=order):
                                for n, piece in enumerate(pieces):
                                    rows = pl.ds((n ^ order) * half, half)
                                    pltpu.make_async_copy(piece.at[:, span], buf.at[rows], sem).start()

        def wait():
            whole = query[0][0] if is_query else keyval[0]
            pltpu.make_async_copy(whole.at[:, span], buf, sem).wait()

        return start, wait


def project_kernel(w, pieces, chunks, ctrl, *refs):
    steps = len(pieces)
    hidden, refs = list(refs[: sum(pieces)]), refs[sum(pieces) :]
    count = len(w.arrays())
    w_refs, refs = w.refs(refs[:count]), refs[count:]
    outs, refs = refs[: len(chunks)], refs[len(chunks) :]
    kept, held, buf, sem, h_sem, kept_sem = refs
    which = ctrl[steps + 1]
    loads = []
    for s, n in enumerate(pieces):
        first, group = 0, []
        for ref in [hidden.pop(0) for _ in range(n)]:
            rows = ref.shape[0]
            group.append(pltpu.make_async_copy(ref, held.at[s, pl.ds(first, rows)], h_sem.at[s, len(group)]))
            first += rows
        loads.append(group)
    todo = [(block, step) for block in range(w.blocks) for step in range(steps)]
    slots = buf.shape[0]
    copies = [
        w.fetch(w_refs, ctrl[step], which, block, buf.at[i % slots], sem.at[i % slots])
        for i, (block, step) in enumerate(todo)
    ]
    keeps = [w.fetch(w_refs, ctrl[steps], which, block, kept.at[block], kept_sem.at[block]) for block in range(w.blocks)]
    for s, group in enumerate(loads):
        for load in group:
            load.start()
        if s < min(slots - 1, len(todo)):
            copies[s][0]()
    for i in range(steps, min(slots - 1, len(todo))):
        copies[i][0]()
    for i, (block, step) in enumerate(todo):
        if i + slots - 1 < len(todo):
            copies[i + slots - 1][0]()
        if step == steps - 1:
            keeps[block][0]()
        if block == 0:
            for load in loads[step]:
                load.wait()
        copies[i][1]()
        span = slice(block * w.width, (block + 1) * w.width)
        first = 0
        for out, rows in zip(outs, chunks):
            part = jnp.dot(held[step, first : first + rows], buf[i % slots], preferred_element_type=F32)
            if step == 0:
                out[:, span] = part
            else:
                out[:, span] += part
            first += rows
    for _, wait in keeps:
        wait()


def project(ctrl, hidden, w, chunks):
    rows, depth = sum(chunks), hidden[0][0].shape[1]
    pieces = [len(h) for h in hidden]
    steps = len(pieces)
    return pl.pallas_call(
        functools.partial(project_kernel, w, pieces, chunks),
        out_shape=[pltpu.VMEM((r, w.all_cols), F32) for r in chunks]
        + [pltpu.VMEM((w.blocks, depth, w.width), BF16)],
        in_specs=[SMEM] + [HBM] * (sum(pieces) + len(w.arrays())),
        out_specs=[VMEM] * (len(chunks) + 1),
        scratch_shapes=[
            pltpu.VMEM((steps, rows, depth), BF16),
            pltpu.VMEM((4, depth, w.width), BF16),
            pltpu.SemaphoreType.DMA((4,)),
            pltpu.SemaphoreType.DMA((steps, max(pieces))),
            pltpu.SemaphoreType.DMA((w.blocks,)),
        ],
        compiler_params=pltpu.CompilerParams(vmem_limit_bytes=24 * MIB),
        cost_estimate=pl.CostEstimate(
            flops=2 * rows * depth * steps * w.all_cols, bytes_accessed=30_000_000, transcendentals=0
        ),
        name="project",
    )(ctrl, *sum(hidden, []), *w.arrays())


def attend_kernel(heads, kv_heads, head_dim, before, part, kept, raw_in, first_ref, cos_ref, sin_ref, *refs):
    kv_before, refs = refs[: len(before)], refs[len(before) :]
    kv_out, mixed_ref, raw, keys_all, values_all = refs
    rows, earlier = part.shape[0], sum(before)
    blocks, _, width = kept.shape
    group = heads // kv_heads
    q_cols = heads * head_dim
    span = earlier + rows
    top = 0
    for ref, n in zip(kv_before, before):
        for g in range(kv_heads):
            keys_all[g, top : top + n] = ref[:, 2 * g * head_dim : (2 * g + 1) * head_dim]
            values_all[g, top : top + n, :head_dim] = ref[:, (2 * g + 1) * head_dim : (2 * g + 2) * head_dim]
        top += n
    for g in range(kv_heads):
        values_all[g, :, head_dim:] = jnp.ones((span, head_dim), BF16)
    cos, sin = cos_ref[...], sin_ref[...]
    for block in range(blocks)[::-1]:
        cols = slice(block * width, (block + 1) * width)
        raw[:, cols] = raw_in[:, cols] + jnp.dot(part[...], kept[block], preferred_element_type=F32)

    def rotated(first):
        u = raw[:, first : first + head_dim]
        return (u * cos + pltpu.roll(u, head_dim // 2, 1) * sin).astype(BF16)

    for g in range(kv_heads):
        first = 2 * g * head_dim
        key = rotated(q_cols + first)
        value = raw[:, q_cols + first + head_dim : q_cols + first + 2 * head_dim].astype(BF16)
        keys_all[g, earlier:span] = key
        values_all[g, earlier:span, :head_dim] = value
        kv_out[:, first : first + head_dim] = key
        kv_out[:, first + head_dim : first + 2 * head_dim] = value
    row_index = earlier + lax.broadcasted_iota(jnp.int32, (rows, span), 0)
    key_index = lax.broadcasted_iota(jnp.int32, (rows, span), 1)
    allowed = (key_index <= row_index) & (key_index >= first_ref[:, :1])
    scale = math.log2(math.e) / math.sqrt(head_dim)
    for g in range(kv_heads):
        mine = range(g * group, (g + 1) * group)
        query = jnp.concatenate([rotated(h * head_dim) for h in mine], axis=0)
        scores = lax.dot_general(query, keys_all[g], (((1,), (1,)), ((), ())), preferred_element_type=F32)
        scores = jnp.where(allowed[None], scores.reshape(group, rows, span) * scale, -jnp.inf)
        weights = jnp.exp2(scores - jnp.max(scores, axis=2, keepdims=True))
        both = jnp.dot(
            weights.astype(BF16).reshape(group * rows, span), values_all[g], preferred_element_type=F32
        )
        mixed = (both[:, :head_dim] / both[:, head_dim:]).astype(BF16)
        for n, h in enumerate(mine):
            mixed_ref[:, h * head_dim : (h + 1) * head_dim] = mixed[n * rows : (n + 1) * rows]


def attend(part, w, kept, raw, tables, kv_before, head_dim):
    rows, depth = part.shape
    heads, kv_heads = w.q_cols // head_dim, w.kv_cols // (2 * head_dim)
    before = [a.shape[0] for a in kv_before]
    count = sum(before) + rows
    return pl.pallas_call(
        functools.partial(attend_kernel, heads, kv_heads, head_dim, before),
        out_shape=[
            jax.ShapeDtypeStruct((rows, w.kv_cols), BF16),
            jax.ShapeDtypeStruct((rows, w.q_cols), BF16),
        ],
        in_specs=[VMEM] * (6 + len(before)),
        out_specs=[VMEM] * 2,
        scratch_shapes=[
            pltpu.VMEM((rows, w.all_cols), F32),
            pltpu.VMEM((kv_heads, count, head_dim), BF16),
            pltpu.VMEM((kv_heads, count, 2 * head_dim), BF16),
        ],
        compiler_params=pltpu.CompilerParams(vmem_limit_bytes=24 * MIB),
        cost_estimate=pl.CostEstimate(
            flops=2 * rows * depth * w.all_cols + 4 * rows * count * w.q_cols,
            bytes_accessed=15_000_000,
            transcendentals=heads * rows * count,
        ),
        name="attend",
    )(part, kept, raw, *tables, *kv_before)


def place_kernel(tops, tok_rows, more, me_ref, source_ref, *refs):
    blocks, out = refs[: len(refs) - 1 - more], refs[-1]
    rows = out.shape[0]
    peers = len(blocks) // len(tops)
    me = me_ref[0]
    total = refs[len(blocks)][...].astype(F32) if more else None
    for n, block in enumerate(blocks):
        chunk, j = divmod(n, peers)
        base = (me ^ j) * tok_rows + tops[chunk]
        index = lax.broadcasted_iota(jnp.int32, (rows, block.shape[0]), 1)
        onehot = (index == source_ref[:, :1] - base).astype(BF16)
        part = jnp.dot(onehot, block[...], preferred_element_type=F32)
        total = part if total is None else total + part
    out[...] = total.astype(BF16)


def place(me, source, blocks, tops, tok_rows, before=None):
    rows, cols = source.shape[0], blocks[0].shape[1]
    more = [] if before is None else [before]
    step = rows // PLACE_STEPS

    def whole(array):
        return pl.BlockSpec(array.shape, lambda i: (0, 0))

    def strip(width):
        return pl.BlockSpec((step, width), lambda i: (i, 0))

    return pl.pallas_call(
        functools.partial(place_kernel, tops, tok_rows, len(more)),
        grid=(PLACE_STEPS,),
        out_shape=jax.ShapeDtypeStruct((rows, cols), BF16),
        in_specs=[SMEM, strip(source.shape[1])] + [whole(b) for b in blocks] + [strip(cols) for _ in more],
        out_specs=strip(cols),
        compiler_params=pltpu.CompilerParams(vmem_limit_bytes=24 * MIB),
        cost_estimate=pl.CostEstimate(
            flops=2 * rows * cols * sum(b.shape[0] for b in blocks),
            bytes_accessed=8 * rows * cols,
            transcendentals=0,
        ),
        name="place",
    )(me, source, *blocks, *more)


def local(hidden, w_query, w_keyval, seg_lengths, home_pos):
    tok_rows = hidden.shape[0]
    w_rows = w_query.shape[0]
    head_dim = w_keyval.shape[2] // 2
    replicas, columns = lax.axis_size("replica"), lax.axis_size("trow")
    me, my_col, my_group = lax.axis_index("replica"), lax.axis_index("trow"), lax.axis_index("groups")
    flat_keyval = w_keyval.reshape(w_rows, -1)
    total = sum(ROW_CHUNKS)
    chunks = [tok_rows * c // total for c in ROW_CHUNKS]
    tops = [sum(chunks[:n]) for n in range(len(chunks))]

    def swap(block, j):
        return lax.ppermute(block, "replica", [(i, i ^ j) for i in range(replicas)])

    def on(block):
        return lax.ppermute(block, "trow", [(i, (i + 1) % columns) for i in range(columns)])

    small = replicas == 4 and columns == 4
    shard_of = [lax.rem(my_col - k + columns, columns) for k in range(columns)]
    picks = [s ^ me for s in shard_of] if small else shard_of
    ctrl = jnp.stack(picks + [my_group]).astype(jnp.int32)
    rows_of = row_tables(seg_lengths[0], tok_rows, head_dim)
    tables = [[t[top : top + rows] for t in rows_of] for top, rows in zip(tops, chunks)]
    source = home_sources(home_pos, tok_rows, me)
    me_array = me.astype(jnp.int32)[None]
    if small:
        half = w_rows // 2
        h1 = on(hidden)
        mine = swap(lax.dynamic_slice_in_dim(w_query, my_group * half, half, 0), 2)
        query_1, keyval_1 = swap(w_query, 1), swap(flat_keyval, 1)
        h1, mine, keyval_later, ctrl, tables, source, me_array = lax.optimization_barrier(
            (h1, mine, flat_keyval, ctrl, tables, source, me_array)
        )
        h2 = on(h1)
        other = lax.ppermute(mine, "groups", [(0, 1), (1, 0)])
        keyval_2 = swap(keyval_later, 2)
        mine_3 = swap(mine, 1)
        h2, other, keyval_2 = lax.optimization_barrier((h2, other, keyval_2))
        hiddens = [[hidden], [h1], [h2]]
        parts = [on(h2[top : top + rows]) for top, rows in zip(tops, chunks)]
        weights = Weights(
            [[w_query], [query_1], [mine, other], [mine_3, swap(other, 1)]],
            [flat_keyval, keyval_1, keyval_2, swap(keyval_2, 1)],
        )
    else:
        hiddens = [[hidden]]
        for _ in range(columns - 2):
            hiddens.append([on(hiddens[-1][0])])
        parts = [on(hiddens[-1][0][top : top + rows]) for top, rows in zip(tops, chunks)]
        depth = hidden.shape[1]
        all_q = lax.all_gather(w_query, "replica", axis=0, tiled=True)
        all_kv = lax.all_gather(flat_keyval, "replica", axis=0, tiled=True)
        spans = [slice(s * depth, (s + 1) * depth) for s in range(columns)]
        weights = Weights([[all_q[s]] for s in spans], [all_kv[s] for s in spans])
    *raws, kept = project(ctrl, hiddens, weights, chunks)
    kv, mixed = [], []
    for part, raw, table in zip(parts, raws, tables):
        kv_new, mixed_new = attend(part, weights, kept, raw, table, kv, head_dim)
        kv, mixed = kv + [kv_new], mixed + [mixed_new]
    blocks = []
    for n, block in enumerate(mixed):
        if small:
            across = swap(block, 2)
            if n + 1 < len(mixed):
                across, _ = lax.optimization_barrier((across, mixed[n + 1]))
                blocks.append([block, swap(block, 1), across, swap(across, 1)])
            else:
                blocks.append([block, swap(block, 1), across])
        else:
            blocks.append([block] + [swap(block, j) for j in range(1, replicas)])
    source_late, _ = lax.optimization_barrier((source, mixed[-1]))
    placed = place(me_array, source_late, sum(blocks[:-1], []), tops[:-1], tok_rows)
    if small:
        across, placed = lax.optimization_barrier((blocks[-1][2], placed))
        blocks[-1] = blocks[-1][:2] + [across, swap(across, 1)]
    return place(me_array, source_late, blocks[-1], tops[-1:], tok_rows, placed)


def solution(mesh):
    placed = (
        P(("groups", "replica"), "trow"),
        P("replica", "trow"),
        P("replica", "trow", None),
        P(("groups", "replica"), None),
        P("groups"),
    )
    return jax.shard_map(
        local,
        mesh=mesh,
        in_specs=placed,
        out_specs=P(("groups", "replica"), "trow"),
        check_vma=False,
    )
```

```python
import functools
import math

import jax
import jax.numpy as jnp
from jax import lax
from jax.experimental import pallas as pl
from jax.experimental.pallas import tpu as pltpu
from jax.sharding import PartitionSpec as P

rope_base = 500000.0
BF16 = jnp.bfloat16
F32 = jnp.float32
MIB = 1024 * 1024
PLACE_STEPS = 5
LANES = 128
ROW_CHUNKS = (320, 192, 128)
VMEM = pl.BlockSpec(memory_space=pltpu.VMEM)
SMEM = pl.BlockSpec(memory_space=pltpu.SMEM)
HBM = pl.BlockSpec(memory_space=pl.ANY)


def row_tables(lengths_row, count, head_dim):
    seg_ends = jnp.cumsum(lengths_row)
    seg_starts = seg_ends - lengths_row
    row_index = jnp.arange(count, dtype=jnp.int32)
    segment = jnp.sum((row_index[:, None] >= seg_ends[None, :]).astype(jnp.int32), axis=1)
    picked = segment[:, None] == jnp.arange(lengths_row.shape[0], dtype=jnp.int32)[None, :]
    seg_first = jnp.sum(jnp.where(picked, seg_starts[None, :], 0), axis=1)
    position = row_index - seg_first
    half_dim = head_dim // 2
    exponent = jnp.arange(half_dim, dtype=F32) * (2.0 / head_dim)
    frequency = jnp.power(F32(rope_base), -exponent)
    angle = position.astype(F32)[:, None] * frequency[None, :]
    cosine, sine = jnp.cos(angle), jnp.sin(angle)
    return (
        jnp.broadcast_to(seg_first.astype(jnp.int32)[:, None], (count, LANES)),
        jnp.concatenate([cosine, cosine], axis=1),
        jnp.concatenate([-sine, sine], axis=1),
    )


def home_sources(home_pos, tok_rows, me):
    target = home_pos - me * tok_rows
    hit = target[None, :] == jnp.arange(tok_rows, dtype=jnp.int32)[:, None]
    packed = jnp.arange(home_pos.shape[0], dtype=jnp.int32)
    source = jnp.sum(jnp.where(hit, packed[None, :], 0), axis=1).astype(jnp.int32)
    return jnp.broadcast_to(source[:, None], (tok_rows, LANES))


class Weights:
    def __init__(self, query, keyval):
        self.query, self.keyval = query, keyval
        self.depth = keyval[0].shape[0]
        self.q_cols, self.kv_cols = query[0][0].shape[1], keyval[0].shape[1]
        self.all_cols = self.q_cols + self.kv_cols
        self.width = math.gcd(512, self.q_cols, self.kv_cols)
        self.blocks = self.all_cols // self.width

    def arrays(self):
        return [piece for pieces in self.query for piece in pieces] + self.keyval

    def refs(self, flat):
        flat = list(flat)
        query = [[flat.pop(0) for _ in pieces] for pieces in self.query]
        return query, flat

    def fetch(self, refs, pick, which, block, buf, sem):
        query, keyval = refs
        q_blocks = self.q_cols // self.width
        is_query = block < q_blocks
        span = pl.ds((block if is_query else block - q_blocks) * self.width, self.width)

        def start():
            for j in range(len(keyval)):
                pieces = query[j] if is_query else [keyval[j]]

                @pl.when(pick == j)
                def _(pieces=pieces):
                    if len(pieces) == 1:
                        pltpu.make_async_copy(pieces[0].at[:, span], buf, sem).start()
                    else:
                        half = self.depth // 2
                        for order in range(2):
                            @pl.when(which == order)
                            def _(order=order):
                                for n, piece in enumerate(pieces):
                                    rows = pl.ds((n ^ order) * half, half)
                                    pltpu.make_async_copy(piece.at[:, span], buf.at[rows], sem).start()

        def wait():
            whole = query[0][0] if is_query else keyval[0]
            pltpu.make_async_copy(whole.at[:, span], buf, sem).wait()

        return start, wait


def project_kernel(w, pieces, chunks, ctrl, *refs):
    steps = len(pieces)
    hidden, refs = list(refs[: sum(pieces)]), refs[sum(pieces) :]
    count = len(w.arrays())
    w_refs, refs = w.refs(refs[:count]), refs[count:]
    outs, refs = refs[: len(chunks)], refs[len(chunks) :]
    kept, held, buf, sem, h_sem, kept_sem = refs
    which = ctrl[steps + 1]
    loads = []
    for s, n in enumerate(pieces):
        first, group = 0, []
        for ref in [hidden.pop(0) for _ in range(n)]:
            rows = ref.shape[0]
            group.append(pltpu.make_async_copy(ref, held.at[s, pl.ds(first, rows)], h_sem.at[s, len(group)]))
            first += rows
        loads.append(group)
    todo = [(block, step) for block in range(w.blocks) for step in range(steps)]
    slots = buf.shape[0]
    copies = [
        w.fetch(w_refs, ctrl[step], which, block, buf.at[i % slots], sem.at[i % slots])
        for i, (block, step) in enumerate(todo)
    ]
    keeps = [w.fetch(w_refs, ctrl[steps], which, block, kept.at[block], kept_sem.at[block]) for block in range(w.blocks)]
    for s, group in enumerate(loads):
        for load in group:
            load.start()
        if s < min(slots - 1, len(todo)):
            copies[s][0]()
    for i in range(steps, min(slots - 1, len(todo))):
        copies[i][0]()
    for i, (block, step) in enumerate(todo):
        if i + slots - 1 < len(todo):
            copies[i + slots - 1][0]()
        if step == steps - 1:
            keeps[block][0]()
        if block == 0:
            for load in loads[step]:
                load.wait()
        copies[i][1]()
        span = slice(block * w.width, (block + 1) * w.width)
        first = 0
        for out, rows in zip(outs, chunks):
            part = jnp.dot(held[step, first : first + rows], buf[i % slots], preferred_element_type=F32)
            if step == 0:
                out[:, span] = part
            else:
                out[:, span] += part
            first += rows
    for _, wait in keeps:
        wait()


def project(ctrl, hidden, w, chunks):
    rows, depth = sum(chunks), hidden[0][0].shape[1]
    pieces = [len(h) for h in hidden]
    steps = len(pieces)
    return pl.pallas_call(
        functools.partial(project_kernel, w, pieces, chunks),
        out_shape=[pltpu.VMEM((r, w.all_cols), F32) for r in chunks]
        + [pltpu.VMEM((w.blocks, depth, w.width), BF16)],
        in_specs=[SMEM] + [HBM] * (sum(pieces) + len(w.arrays())),
        out_specs=[VMEM] * (len(chunks) + 1),
        scratch_shapes=[
            pltpu.VMEM((steps, rows, depth), BF16),
            pltpu.VMEM((4, depth, w.width), BF16),
            pltpu.SemaphoreType.DMA((4,)),
            pltpu.SemaphoreType.DMA((steps, max(pieces))),
            pltpu.SemaphoreType.DMA((w.blocks,)),
        ],
        compiler_params=pltpu.CompilerParams(vmem_limit_bytes=24 * MIB),
        cost_estimate=pl.CostEstimate(
            flops=2 * rows * depth * steps * w.all_cols, bytes_accessed=30_000_000, transcendentals=0
        ),
        name="project",
    )(ctrl, *sum(hidden, []), *w.arrays())


def attend_kernel(heads, kv_heads, head_dim, before, part, kept, raw_in, first_ref, cos_ref, sin_ref, *refs):
    kv_before, refs = refs[: len(before)], refs[len(before) :]
    kv_out, mixed_ref, raw, keys_all, values_all = refs
    rows, earlier = part.shape[0], sum(before)
    blocks, _, width = kept.shape
    group = heads // kv_heads
    q_cols = heads * head_dim
    span = earlier + rows
    top = 0
    for ref, n in zip(kv_before, before):
        for g in range(kv_heads):
            keys_all[g, top : top + n] = ref[:, 2 * g * head_dim : (2 * g + 1) * head_dim]
            values_all[g, top : top + n, :head_dim] = ref[:, (2 * g + 1) * head_dim : (2 * g + 2) * head_dim]
        top += n
    for g in range(kv_heads):
        values_all[g, :, head_dim:] = jnp.ones((span, head_dim), BF16)
    cos, sin = cos_ref[...], sin_ref[...]
    for block in range(blocks)[::-1]:
        cols = slice(block * width, (block + 1) * width)
        raw[:, cols] = raw_in[:, cols] + jnp.dot(part[...], kept[block], preferred_element_type=F32)

    def rotated(first):
        u = raw[:, first : first + head_dim]
        return (u * cos + pltpu.roll(u, head_dim // 2, 1) * sin).astype(BF16)

    for g in range(kv_heads):
        first = 2 * g * head_dim
        key = rotated(q_cols + first)
        value = raw[:, q_cols + first + head_dim : q_cols + first + 2 * head_dim].astype(BF16)
        keys_all[g, earlier:span] = key
        values_all[g, earlier:span, :head_dim] = value
        kv_out[:, first : first + head_dim] = key
        kv_out[:, first + head_dim : first + 2 * head_dim] = value
    row_index = earlier + lax.broadcasted_iota(jnp.int32, (rows, span), 0)
    key_index = lax.broadcasted_iota(jnp.int32, (rows, span), 1)
    allowed = (key_index <= row_index) & (key_index >= first_ref[:, :1])
    scale = math.log2(math.e) / math.sqrt(head_dim)
    for g in range(kv_heads):
        mine = range(g * group, (g + 1) * group)
        query = jnp.concatenate([rotated(h * head_dim) for h in mine], axis=0)
        scores = lax.dot_general(query, keys_all[g], (((1,), (1,)), ((), ())), preferred_element_type=F32)
        scores = jnp.where(allowed[None], scores.reshape(group, rows, span) * scale, -jnp.inf)
        weights = jnp.exp2(scores - jnp.max(scores, axis=2, keepdims=True))
        both = jnp.dot(
            weights.astype(BF16).reshape(group * rows, span), values_all[g], preferred_element_type=F32
        )
        mixed = (both[:, :head_dim] / both[:, head_dim:]).astype(BF16)
        for n, h in enumerate(mine):
            mixed_ref[:, h * head_dim : (h + 1) * head_dim] = mixed[n * rows : (n + 1) * rows]


def attend(part, w, kept, raw, tables, kv_before, head_dim):
    rows, depth = part.shape
    heads, kv_heads = w.q_cols // head_dim, w.kv_cols // (2 * head_dim)
    before = [a.shape[0] for a in kv_before]
    count = sum(before) + rows
    return pl.pallas_call(
        functools.partial(attend_kernel, heads, kv_heads, head_dim, before),
        out_shape=[
            jax.ShapeDtypeStruct((rows, w.kv_cols), BF16),
            jax.ShapeDtypeStruct((rows, w.q_cols), BF16),
        ],
        in_specs=[VMEM] * (6 + len(before)),
        out_specs=[VMEM] * 2,
        scratch_shapes=[
            pltpu.VMEM((rows, w.all_cols), F32),
            pltpu.VMEM((kv_heads, count, head_dim), BF16),
            pltpu.VMEM((kv_heads, count, 2 * head_dim), BF16),
        ],
        compiler_params=pltpu.CompilerParams(vmem_limit_bytes=24 * MIB),
        cost_estimate=pl.CostEstimate(
            flops=2 * rows * depth * w.all_cols + 4 * rows * count * w.q_cols,
            bytes_accessed=15_000_000,
            transcendentals=heads * rows * count,
        ),
        name="attend",
    )(part, kept, raw, *tables, *kv_before)


def place_kernel(spans, tok_rows, more, final, me_ref, source_ref, *refs):
    blocks, refs = refs[: len(spans)], refs[len(spans) :]
    before, refs = refs[:more], refs[more:]
    out = refs[0]
    rows = source_ref.shape[0]
    step = rows // PLACE_STEPS
    me = me_ref[0]
    writes = []
    for i in range(PLACE_STEPS):
        strip = slice(i * step, (i + 1) * step)
        total = before[0][strip].astype(F32) if more else None
        for block, parts in zip(blocks, spans):
            for first, count, j, top in parts:
                base = (me ^ j) * tok_rows + top
                index = lax.broadcasted_iota(jnp.int32, (step, count), 1)
                onehot = (index == source_ref[strip, :1] - base).astype(BF16)
                part = jnp.dot(onehot, block[first : first + count], preferred_element_type=F32)
                total = part if total is None else total + part
        if final:
            held, sem = refs[1:]
            held[strip] = total.astype(BF16)
            span = pl.ds(i * step, step)
            writes.append(pltpu.make_async_copy(held.at[span], out.at[span], sem.at[i]))
            writes[-1].start()
        else:
            out[strip] = total.astype(BF16)
    for write in writes:
        write.wait()


def place(me, source, arrived, tok_rows, before=None):
    blocks, spans = [a for a, _ in arrived], [p for _, p in arrived]
    rows, cols = source.shape[0], blocks[0].shape[1]
    more = [] if before is None else [before]
    final = len(more)
    scratch = [pltpu.VMEM((rows, cols), BF16), pltpu.SemaphoreType.DMA((PLACE_STEPS,))]
    return pl.pallas_call(
        functools.partial(place_kernel, spans, tok_rows, len(more), final),
        out_shape=jax.ShapeDtypeStruct((rows, cols), BF16),
        in_specs=[SMEM] + [VMEM] * (1 + len(blocks) + len(more)),
        out_specs=HBM if final else VMEM,
        scratch_shapes=scratch if final else [],
        compiler_params=pltpu.CompilerParams(vmem_limit_bytes=24 * MIB),
        cost_estimate=pl.CostEstimate(
            flops=2 * rows * cols * sum(b.shape[0] for b in blocks),
            bytes_accessed=8 * rows * cols,
            transcendentals=0,
        ),
        name="place",
    )(me, source, *blocks, *more)


def local(hidden, w_query, w_keyval, seg_lengths, home_pos):
    tok_rows = hidden.shape[0]
    w_rows = w_query.shape[0]
    head_dim = w_keyval.shape[2] // 2
    replicas, columns = lax.axis_size("replica"), lax.axis_size("trow")
    me, my_col, my_group = lax.axis_index("replica"), lax.axis_index("trow"), lax.axis_index("groups")
    flat_keyval = w_keyval.reshape(w_rows, -1)
    total = sum(ROW_CHUNKS)
    chunks = [tok_rows * c // total for c in ROW_CHUNKS]
    tops = [sum(chunks[:n]) for n in range(len(chunks))]

    def swap(block, j):
        return lax.ppermute(block, "replica", [(i, i ^ j) for i in range(replicas)])

    def after(block, *others):
        return lax.optimization_barrier((block, *others))[0]

    def on(block):
        return lax.ppermute(block, "trow", [(i, (i + 1) % columns) for i in range(columns)])

    small = replicas == 4 and columns == 4
    shard_of = [lax.rem(my_col - k + columns, columns) for k in range(columns)]
    picks = [s ^ me for s in shard_of] if small else shard_of
    ctrl = jnp.stack(picks + [my_group]).astype(jnp.int32)
    rows_of = row_tables(seg_lengths[0], tok_rows, head_dim)
    tables = [[t[top : top + rows] for t in rows_of] for top, rows in zip(tops, chunks)]
    source = home_sources(home_pos, tok_rows, me)
    me_array = me.astype(jnp.int32)[None]
    if small:
        half = w_rows // 2
        h1 = on(hidden)
        mine = swap(lax.dynamic_slice_in_dim(w_query, my_group * half, half, 0), 2)
        query_1, keyval_1 = swap(w_query, 1), swap(flat_keyval, 1)
        mine, ctrl, tables, source, me_array = lax.optimization_barrier((mine, ctrl, tables, source, me_array))
        h1, mine, keyval_later = lax.optimization_barrier((h1, mine, flat_keyval))
        h2 = on(h1)
        other = lax.ppermute(mine, "groups", [(0, 1), (1, 0)])
        keyval_2 = swap(keyval_later, 2)
        mine_3 = swap(mine, 1)
        hiddens = [[hidden], [h1], [h2]]
        parts = [on(h2[top : top + rows]) for top, rows in zip(tops, chunks)]
        weights = Weights(
            [[w_query], [query_1], [mine, other], [mine_3, swap(other, 1)]],
            [flat_keyval, keyval_1, keyval_2, swap(keyval_2, 1)],
        )
    else:
        hiddens = [[hidden]]
        for _ in range(columns - 2):
            hiddens.append([on(hiddens[-1][0])])
        parts = [on(hiddens[-1][0][top : top + rows]) for top, rows in zip(tops, chunks)]
        depth = hidden.shape[1]
        all_q = lax.all_gather(w_query, "replica", axis=0, tiled=True)
        all_kv = lax.all_gather(flat_keyval, "replica", axis=0, tiled=True)
        spans = [slice(s * depth, (s + 1) * depth) for s in range(columns)]
        weights = Weights([[all_q[s]] for s in spans], [all_kv[s] for s in spans])
    *raws, kept = project(ctrl, hiddens, weights, chunks)
    kv, mixed = [], []
    for part, raw, table in zip(parts, raws, tables):
        kv_new, mixed_new = attend(part, weights, kept, raw, table, kv, head_dim)
        kv, mixed = kv + [kv_new], mixed + [mixed_new]
    last = len(mixed) - 1
    early, late = [], []
    for n, (block, top, rows) in enumerate(zip(mixed, tops, chunks)):
        if not small:
            arrived = [swap(block, j) if j else block for j in range(replicas)]
        else:
            across = swap(block, 2)
            arrived = [block, swap(block, 1), across]
            if n < last:
                arrived[2] = after(across, mixed[n + 1])
                arrived.append(swap(arrived[2], 1))
        (late if n == last else early).extend((a, [(0, rows, j, top)]) for j, a in enumerate(arrived))
    source_late = after(source, mixed[last])
    placed = place(me_array, source_late, early, tok_rows)
    if small:
        final, placed = lax.optimization_barrier((late[2][0], placed))
        late[2] = (final, late[2][1])
        late.append((swap(final, 1), [(0, chunks[last], 3, tops[last])]))
    return place(me_array, source_late, late, tok_rows, placed)


def solution(mesh):
    placed = (
        P(("groups", "replica"), "trow"),
        P("replica", "trow"),
        P("replica", "trow", None),
        P(("groups", "replica"), None),
        P("groups"),
    )
    return jax.shard_map(
        local,
        mesh=mesh,
        in_specs=placed,
        out_specs=P(("groups", "replica"), "trow"),
        check_vma=False,
    )
```

```python
import functools
import math

import jax
import jax.numpy as jnp
from jax import lax
from jax.experimental import pallas as pl
from jax.experimental.pallas import tpu as pltpu
from jax.sharding import PartitionSpec as P

rope_base = 500000.0
BF16 = jnp.bfloat16
F32 = jnp.float32
MIB = 1024 * 1024
PLACE_STEPS = 5
LANES = 128
ROW_CHUNKS = (320, 192, 128)
VMEM = pl.BlockSpec(memory_space=pltpu.VMEM)
SMEM = pl.BlockSpec(memory_space=pltpu.SMEM)
HBM = pl.BlockSpec(memory_space=pl.ANY)


def row_tables(lengths_row, count, head_dim):
    seg_ends = jnp.cumsum(lengths_row)
    seg_starts = seg_ends - lengths_row
    row_index = jnp.arange(count, dtype=jnp.int32)
    segment = jnp.sum((row_index[:, None] >= seg_ends[None, :]).astype(jnp.int32), axis=1)
    picked = segment[:, None] == jnp.arange(lengths_row.shape[0], dtype=jnp.int32)[None, :]
    seg_first = jnp.sum(jnp.where(picked, seg_starts[None, :], 0), axis=1)
    position = row_index - seg_first
    half_dim = head_dim // 2
    exponent = jnp.arange(half_dim, dtype=F32) * (2.0 / head_dim)
    frequency = jnp.power(F32(rope_base), -exponent)
    angle = position.astype(F32)[:, None] * frequency[None, :]
    cosine, sine = jnp.cos(angle), jnp.sin(angle)
    return (
        jnp.broadcast_to(seg_first.astype(jnp.int32)[:, None], (count, LANES)),
        jnp.concatenate([cosine, cosine], axis=1),
        jnp.concatenate([-sine, sine], axis=1),
    )


def home_sources(home_pos, tok_rows, me):
    target = home_pos - me * tok_rows
    hit = target[None, :] == jnp.arange(tok_rows, dtype=jnp.int32)[:, None]
    packed = jnp.arange(home_pos.shape[0], dtype=jnp.int32)
    source = jnp.sum(jnp.where(hit, packed[None, :], 0), axis=1).astype(jnp.int32)
    return jnp.broadcast_to(source[:, None], (tok_rows, LANES))


class Weights:
    def __init__(self, query, keyval):
        self.query, self.keyval = query, keyval
        self.depth = keyval[0].shape[0]
        self.q_cols, self.kv_cols = query[0][0].shape[1], keyval[0].shape[1]
        self.all_cols = self.q_cols + self.kv_cols
        self.width = math.gcd(512, self.q_cols, self.kv_cols)
        self.blocks = self.all_cols // self.width

    def arrays(self):
        return [piece for pieces in self.query for piece in pieces] + self.keyval

    def refs(self, flat):
        flat = list(flat)
        query = [[flat.pop(0) for _ in pieces] for pieces in self.query]
        return query, flat

    def fetch(self, refs, pick, which, block, buf, sem):
        query, keyval = refs
        q_blocks = self.q_cols // self.width
        is_query = block < q_blocks
        span = pl.ds((block if is_query else block - q_blocks) * self.width, self.width)

        def start():
            for j in range(len(keyval)):
                pieces = query[j] if is_query else [keyval[j]]

                @pl.when(pick == j)
                def _(pieces=pieces):
                    if len(pieces) == 1:
                        pltpu.make_async_copy(pieces[0].at[:, span], buf, sem).start()
                    else:
                        half = self.depth // 2
                        for order in range(2):
                            @pl.when(which == order)
                            def _(order=order):
                                for n, piece in enumerate(pieces):
                                    rows = pl.ds((n ^ order) * half, half)
                                    pltpu.make_async_copy(piece.at[:, span], buf.at[rows], sem).start()

        def wait():
            whole = query[0][0] if is_query else keyval[0]
            pltpu.make_async_copy(whole.at[:, span], buf, sem).wait()

        return start, wait


def project_kernel(w, pieces, chunks, ctrl, *refs):
    steps = len(pieces)
    hidden, refs = list(refs[: sum(pieces)]), refs[sum(pieces) :]
    count = len(w.arrays())
    w_refs, refs = w.refs(refs[:count]), refs[count:]
    outs, refs = refs[: len(chunks)], refs[len(chunks) :]
    kept, held, buf, sem, h_sem, kept_sem = refs
    which = ctrl[steps + 1]
    loads = []
    for s, n in enumerate(pieces):
        first, group = 0, []
        for ref in [hidden.pop(0) for _ in range(n)]:
            rows = ref.shape[0]
            group.append(pltpu.make_async_copy(ref, held.at[s, pl.ds(first, rows)], h_sem.at[s, len(group)]))
            first += rows
        loads.append(group)
    todo = [(block, step) for block in range(w.blocks) for step in range(steps)]
    slots = buf.shape[0]
    copies = [
        w.fetch(w_refs, ctrl[step], which, block, buf.at[i % slots], sem.at[i % slots])
        for i, (block, step) in enumerate(todo)
    ]
    keeps = [w.fetch(w_refs, ctrl[steps], which, block, kept.at[block], kept_sem.at[block]) for block in range(w.blocks)]
    for s, group in enumerate(loads):
        for load in group:
            load.start()
        if s < min(slots - 1, len(todo)):
            copies[s][0]()
    for i in range(steps, min(slots - 1, len(todo))):
        copies[i][0]()
    for i, (block, step) in enumerate(todo):
        if i + slots - 1 < len(todo):
            copies[i + slots - 1][0]()
        if step == steps - 1:
            keeps[block][0]()
        if block == 0:
            for load in loads[step]:
                load.wait()
        copies[i][1]()
        span = slice(block * w.width, (block + 1) * w.width)
        first = 0
        for out, rows in zip(outs, chunks):
            part = jnp.dot(held[step, first : first + rows], buf[i % slots], preferred_element_type=F32)
            if step == 0:
                out[:, span] = part
            else:
                out[:, span] += part
            first += rows
    for _, wait in keeps:
        wait()


def project(ctrl, hidden, w, chunks):
    rows, depth = sum(chunks), hidden[0][0].shape[1]
    pieces = [len(h) for h in hidden]
    steps = len(pieces)
    return pl.pallas_call(
        functools.partial(project_kernel, w, pieces, chunks),
        out_shape=[pltpu.VMEM((r, w.all_cols), F32) for r in chunks]
        + [pltpu.VMEM((w.blocks, depth, w.width), BF16)],
        in_specs=[SMEM] + [HBM] * (sum(pieces) + len(w.arrays())),
        out_specs=[VMEM] * (len(chunks) + 1),
        scratch_shapes=[
            pltpu.VMEM((steps, rows, depth), BF16),
            pltpu.VMEM((4, depth, w.width), BF16),
            pltpu.SemaphoreType.DMA((4,)),
            pltpu.SemaphoreType.DMA((steps, max(pieces))),
            pltpu.SemaphoreType.DMA((w.blocks,)),
        ],
        compiler_params=pltpu.CompilerParams(vmem_limit_bytes=24 * MIB),
        cost_estimate=pl.CostEstimate(
            flops=2 * rows * depth * steps * w.all_cols, bytes_accessed=30_000_000, transcendentals=0
        ),
        name="project",
    )(ctrl, *sum(hidden, []), *w.arrays())


def attend_kernel(heads, kv_heads, head_dim, before, part, kept, raw_in, first_ref, cos_ref, sin_ref, *refs):
    kv_before, refs = refs[: len(before)], refs[len(before) :]
    kv_out, mixed_ref, raw, keys_all, values_all = refs
    rows, earlier = part.shape[0], sum(before)
    blocks, _, width = kept.shape
    group = heads // kv_heads
    q_cols = heads * head_dim
    span = earlier + rows
    top = 0
    for ref, n in zip(kv_before, before):
        for g in range(kv_heads):
            keys_all[g, top : top + n] = ref[:, 2 * g * head_dim : (2 * g + 1) * head_dim]
            values_all[g, top : top + n, :head_dim] = ref[:, (2 * g + 1) * head_dim : (2 * g + 2) * head_dim]
        top += n
    for g in range(kv_heads):
        values_all[g, :, head_dim:] = jnp.ones((span, head_dim), BF16)
    cos, sin = cos_ref[...], sin_ref[...]
    for block in range(blocks)[::-1]:
        cols = slice(block * width, (block + 1) * width)
        raw[:, cols] = raw_in[:, cols] + jnp.dot(part[...], kept[block], preferred_element_type=F32)

    def rotated(first):
        u = raw[:, first : first + head_dim]
        return (u * cos + pltpu.roll(u, head_dim // 2, 1) * sin).astype(BF16)

    for g in range(kv_heads):
        first = 2 * g * head_dim
        key = rotated(q_cols + first)
        value = raw[:, q_cols + first + head_dim : q_cols + first + 2 * head_dim].astype(BF16)
        keys_all[g, earlier:span] = key
        values_all[g, earlier:span, :head_dim] = value
        kv_out[:, first : first + head_dim] = key
        kv_out[:, first + head_dim : first + 2 * head_dim] = value
    row_index = earlier + lax.broadcasted_iota(jnp.int32, (rows, span), 0)
    key_index = lax.broadcasted_iota(jnp.int32, (rows, span), 1)
    allowed = (key_index <= row_index) & (key_index >= first_ref[:, :1])
    scale = math.log2(math.e) / math.sqrt(head_dim)
    for g in range(kv_heads):
        mine = range(g * group, (g + 1) * group)
        query = jnp.concatenate([rotated(h * head_dim) for h in mine], axis=0)
        scores = lax.dot_general(query, keys_all[g], (((1,), (1,)), ((), ())), preferred_element_type=F32)
        scores = jnp.where(allowed[None], scores.reshape(group, rows, span) * scale, -jnp.inf)
        weights = jnp.exp2(scores - jnp.max(scores, axis=2, keepdims=True))
        both = jnp.dot(
            weights.astype(BF16).reshape(group * rows, span), values_all[g], preferred_element_type=F32
        )
        mixed = (both[:, :head_dim] / both[:, head_dim:]).astype(BF16)
        for n, h in enumerate(mine):
            mixed_ref[:, h * head_dim : (h + 1) * head_dim] = mixed[n * rows : (n + 1) * rows]


def attend(part, w, kept, raw, tables, kv_before, head_dim):
    rows, depth = part.shape
    heads, kv_heads = w.q_cols // head_dim, w.kv_cols // (2 * head_dim)
    before = [a.shape[0] for a in kv_before]
    count = sum(before) + rows
    return pl.pallas_call(
        functools.partial(attend_kernel, heads, kv_heads, head_dim, before),
        out_shape=[
            jax.ShapeDtypeStruct((rows, w.kv_cols), BF16),
            jax.ShapeDtypeStruct((rows, w.q_cols), BF16),
        ],
        in_specs=[VMEM] * (6 + len(before)),
        out_specs=[VMEM] * 2,
        scratch_shapes=[
            pltpu.VMEM((rows, w.all_cols), F32),
            pltpu.VMEM((kv_heads, count, head_dim), BF16),
            pltpu.VMEM((kv_heads, count, 2 * head_dim), BF16),
        ],
        compiler_params=pltpu.CompilerParams(vmem_limit_bytes=24 * MIB),
        cost_estimate=pl.CostEstimate(
            flops=2 * rows * depth * w.all_cols + 4 * rows * count * w.q_cols,
            bytes_accessed=15_000_000,
            transcendentals=heads * rows * count,
        ),
        name="attend",
    )(part, kept, raw, *tables, *kv_before)


def place_kernel(spans, tok_rows, more, final, me_ref, source_ref, *refs):
    blocks, refs = refs[: len(spans)], refs[len(spans) :]
    before, refs = refs[:more], refs[more:]
    out = refs[0]
    rows = source_ref.shape[0]
    step = rows // PLACE_STEPS
    me = me_ref[0]
    writes = []
    for i in range(PLACE_STEPS):
        strip = slice(i * step, (i + 1) * step)
        total = before[0][strip].astype(F32) if more else None
        for block, parts in zip(blocks, spans):
            for first, count, j, top in parts:
                base = (me ^ j) * tok_rows + top
                index = lax.broadcasted_iota(jnp.int32, (step, count), 1)
                onehot = (index == source_ref[strip, :1] - base).astype(BF16)
                part = jnp.dot(onehot, block[first : first + count], preferred_element_type=F32)
                total = part if total is None else total + part
        if final:
            held, sem = refs[1:]
            held[strip] = total.astype(BF16)
            span = pl.ds(i * step, step)
            writes.append(pltpu.make_async_copy(held.at[span], out.at[span], sem.at[i]))
            writes[-1].start()
        else:
            out[strip] = total.astype(BF16)
    for write in writes:
        write.wait()


def place(me, source, arrived, tok_rows, before=None):
    blocks, spans = [a for a, _ in arrived], [p for _, p in arrived]
    rows, cols = source.shape[0], blocks[0].shape[1]
    more = [] if before is None else [before]
    final = len(more)
    scratch = [pltpu.VMEM((rows, cols), BF16), pltpu.SemaphoreType.DMA((PLACE_STEPS,))]
    return pl.pallas_call(
        functools.partial(place_kernel, spans, tok_rows, len(more), final),
        out_shape=jax.ShapeDtypeStruct((rows, cols), BF16),
        in_specs=[SMEM] + [VMEM] * (1 + len(blocks) + len(more)),
        out_specs=HBM if final else VMEM,
        scratch_shapes=scratch if final else [],
        compiler_params=pltpu.CompilerParams(vmem_limit_bytes=24 * MIB),
        cost_estimate=pl.CostEstimate(
            flops=2 * rows * cols * sum(b.shape[0] for b in blocks),
            bytes_accessed=8 * rows * cols,
            transcendentals=0,
        ),
        name="place",
    )(me, source, *blocks, *more)


def local(hidden, w_query, w_keyval, seg_lengths, home_pos):
    tok_rows = hidden.shape[0]
    w_rows = w_query.shape[0]
    head_dim = w_keyval.shape[2] // 2
    replicas, columns = lax.axis_size("replica"), lax.axis_size("trow")
    me, my_col, my_group = lax.axis_index("replica"), lax.axis_index("trow"), lax.axis_index("groups")
    flat_keyval = w_keyval.reshape(w_rows, -1)
    total = sum(ROW_CHUNKS)
    chunks = [tok_rows * c // total for c in ROW_CHUNKS]
    tops = [sum(chunks[:n]) for n in range(len(chunks))]

    def swap(block, j):
        return lax.ppermute(block, "replica", [(i, i ^ j) for i in range(replicas)])

    def after(block, *others):
        return lax.optimization_barrier((block, *others))[0]

    def on(block):
        return lax.ppermute(block, "trow", [(i, (i + 1) % columns) for i in range(columns)])

    small = replicas == 4 and columns == 4
    shard_of = [lax.rem(my_col - k + columns, columns) for k in range(columns)]
    picks = [s ^ me for s in shard_of] if small else shard_of
    ctrl = jnp.stack(picks + [my_group]).astype(jnp.int32)
    rows_of = row_tables(seg_lengths[0], tok_rows, head_dim)
    tables = [[t[top : top + rows] for t in rows_of] for top, rows in zip(tops, chunks)]
    source = home_sources(home_pos, tok_rows, me)
    me_array = me.astype(jnp.int32)[None]
    if small:
        half = w_rows // 2
        h1 = on(hidden)
        mine = swap(lax.dynamic_slice_in_dim(w_query, my_group * half, half, 0), 2)
        query_1, keyval_1 = swap(w_query, 1), swap(flat_keyval, 1)
        mine, ctrl, tables, source, me_array = lax.optimization_barrier((mine, ctrl, tables, source, me_array))
        h1, mine, keyval_later = lax.optimization_barrier((h1, mine, flat_keyval))
        h2 = on(h1)
        other = lax.ppermute(mine, "groups", [(0, 1), (1, 0)])
        keyval_2 = swap(keyval_later, 2)
        mine_3 = swap(mine, 1)
        hiddens = [[hidden], [h1], [h2]]
        parts = [on(h2[top : top + rows]) for top, rows in zip(tops, chunks)]
        weights = Weights(
            [[w_query], [query_1], [mine, other], [mine_3, swap(other, 1)]],
            [flat_keyval, keyval_1, keyval_2, swap(keyval_2, 1)],
        )
    else:
        hiddens = [[hidden]]
        for _ in range(columns - 2):
            hiddens.append([on(hiddens[-1][0])])
        parts = [on(hiddens[-1][0][top : top + rows]) for top, rows in zip(tops, chunks)]
        depth = hidden.shape[1]
        all_q = lax.all_gather(w_query, "replica", axis=0, tiled=True)
        all_kv = lax.all_gather(flat_keyval, "replica", axis=0, tiled=True)
        spans = [slice(s * depth, (s + 1) * depth) for s in range(columns)]
        weights = Weights([[all_q[s]] for s in spans], [all_kv[s] for s in spans])
    *raws, kept = project(ctrl, hiddens, weights, chunks)
    kv, mixed = [], []
    for part, raw, table in zip(parts, raws, tables):
        kv_new, mixed_new = attend(part, weights, kept, raw, table, kv, head_dim)
        kv, mixed = kv + [kv_new], mixed + [mixed_new]
    last = len(mixed) - 1
    early = []
    for n, (block, top, rows) in enumerate(zip(mixed, tops, chunks)):
        if not small:
            arrived = [swap(block, j) if j else block for j in range(replicas)]
        else:
            across = swap(block, 2)
            arrived = [block, swap(block, 1), across]
            if n < last:
                arrived[2] = after(across, mixed[n + 1])
                arrived.append(swap(arrived[2], 1))
        arrived = [(a, [(0, rows, j, top)]) for j, a in enumerate(arrived)]
        early += arrived if n < last else arrived[:1]
        late = arrived[1:]
    source_late = after(source, mixed[last])
    placed = place(me_array, source_late, early, tok_rows)
    if small:
        final, placed = lax.optimization_barrier((late[1][0], placed))
        late = [late[0], (final, late[1][1]), (swap(final, 1), [(0, chunks[last], 3, tops[last])])]
    return place(me_array, source_late, late, tok_rows, placed)


def solution(mesh):
    placed = (
        P(("groups", "replica"), "trow"),
        P("replica", "trow"),
        P("replica", "trow", None),
        P(("groups", "replica"), None),
        P("groups"),
    )
    return jax.shard_map(
        local,
        mesh=mesh,
        in_specs=placed,
        out_specs=P(("groups", "replica"), "trow"),
        check_vma=False,
    )
```
